32 devices in a mesh: seq: 8 (over y, x, core), mp: 4 (over z).
Axes of the slice: x: 2, y: 2, z: 4, core: 2. Of those that a mesh axis runs over, the one named last changes fastest.
Arguments:
- query_latent: bfloat16 [2048, 1536], P(('seq', 'mp')), may hold values from -6 to 6
- new_kv: bfloat16 [2048, 576], P(('seq', 'mp')), may hold values from -6 to 6
- q_weight: bfloat16 [1536, 24576], P('seq', 'mp'), may hold values from -0.15625 to 0.15625
- q_scales: float32 [12, 192], P(None, 'mp'), may hold values from 0.5 to 2
- kv_weight: bfloat16 [32768, 512], P(('mp', 'seq')), may hold values from -0.5 to 0.5
- kv_scales: float32 [256, 4], P('mp'), may hold values from 0.5 to 2
- kv_gain: float32 [512], replicated, may hold values from 0.1 to 1.9
- pool_latent: bfloat16 [128, 64, 512], P('seq'), may hold values from -64 to 64
- pool_rope: bfloat16 [128, 4096], P('seq'), may hold values from -6 to 6
- page_table: int32 [8, 16], replicated, may hold values from 0 to 127, as said below
- prior_len: int32 [8], replicated, may hold values from 1 to 1024, as said below
Outputs:
- attended: bfloat16 [2048, 16384], P('seq', 'mp')
The draws below stay inside these ranges and needn't reach their ends.
Inputs may be any that keep to these rules, and one draw needn't show every extreme that they name: `page_table`: pool pages 16 * d to 16 * d + 15 sit on seq device d, and reply r's tokens on seq device r. Every pool page serves exactly one (reply, page) pair. Page j of every reply r lies on device (r + o_j) mod 8 for offsets o_j common to all replies. No device holds more than 2 pages of one reply, and in every draw some device holds exactly 2 pages of each reply. `prior_len`: some reply reaches the most.
All inputs are finite; a program needn't handle non-finite values.
Results may differ from the reference program's by a relative error of at most 0.009.
The reference program's roundings to bfloat16 on the way count: a program that leaves them out, or rounds other values in their place, can miss the bound.
Values may be sent and summed in bfloat16 or wider, within the bound.
A program may use at most 192 MiB of HBM per device.

```python
import math
import jax
import jax.numpy as jnp
from jax import lax

QLORA = 1536
HEADS = 128
NOPE = 128
ROPE = 64
VDIM = 128
LATENT = 512
BLOCK = 128
PAGE = 64
REPLY_TOK = 256
PAGES = 16
REPLIES = 8
TOKENS = 2048
POOL = 128
QCOLS = 24576
KVROWS = 32768
N_SEQ = 8


def draw_page_table(key, part):
    key_shift, key_slot = jax.random.split(jax.random.fold_in(key, 11))
    order = jax.random.permutation(key_shift, N_SEQ)
    offsets = order[jnp.arange(PAGES) % N_SEQ]
    holders = (jnp.arange(REPLIES)[:, None] + offsets[None, :]) % N_SEQ
    slot_orders = jax.vmap(lambda sub_key: jax.random.permutation(sub_key, PAGES))(jax.random.split(key_slot, N_SEQ))
    local_slot = slot_orders[holders, jnp.arange(PAGES)[None, :]]
    return (holders * PAGES + local_slot).astype(jnp.int32)


def draw_prior_len(key, part):
    key_one, key_two, key_pick = jax.random.split(jax.random.fold_in(key, 23), 3)
    longest = PAGES * PAGE
    first_draw = jax.random.randint(key_one, (REPLIES,), 1, longest + 1)
    second_draw = jax.random.randint(key_two, (REPLIES,), 1, longest + 1)
    lengths = jnp.minimum(first_draw, second_draw)
    chosen = jax.random.randint(key_pick, (), 0, REPLIES)
    return jnp.where(jnp.arange(REPLIES) == chosen, longest, lengths).astype(jnp.int32)


def draw_pool_latent(key, part):
    key_base = jax.random.fold_in(jax.random.fold_in(key, 31), 0)
    full_shape = (POOL, PAGE, LATENT)
    values = jnp.clip(jax.random.normal(key_base, full_shape, jnp.float32), -6.0, 6.0)
    return values.astype(jnp.bfloat16)


def shard_levels(rng, dims, cuts, least, high):
    loudness = 1.0
    for axis_at, shards_of in cuts:
        heights = jax.random.uniform(jax.random.fold_in(jax.random.fold_in(rng, 6), axis_at), (shards_of,), jnp.float32, least / len(cuts), high / len(cuts))
        loudness = loudness * jnp.repeat(jnp.exp(heights), dims[axis_at] // shards_of).reshape((-1,) + (1,) * (len(dims) - 1 - axis_at))
    return loudness


def normal_values(rng, dims, spread, limit, cuts=(), kind=jnp.bfloat16):
    drawn = jax.random.normal(rng, dims, jnp.float32) * spread
    if len(cuts) > 0:
        drawn = shard_levels(rng, dims, cuts, -0.22, 0.18) * drawn
    return jnp.clip(drawn, min=-limit, max=limit).astype(kind)


def setup_inputs(seed: int = 0) -> dict:
    key_list = jax.random.split(jax.random.key(seed), 12)
    query_latent = normal_values(key_list[0], (TOKENS, QLORA), 1.0, 6.0, ((0, 32),))
    new_kv = normal_values(key_list[1], (TOKENS, LATENT + ROPE), 1.0, 6.0, ((0, 32),))
    q_weight = normal_values(key_list[2], (QLORA, QCOLS), QLORA ** -0.5, 0.15625, ((0, 8), (1, 4)))
    q_scales = jnp.clip(jnp.exp(math.log(2.0) - 1.3862944 * jax.random.uniform(key_list[3], (QLORA // BLOCK, QCOLS // BLOCK), jnp.float32) ** shard_levels(key_list[3], (QLORA // BLOCK, QCOLS // BLOCK), ((1, 4),), -0.2, 0.2)), 0.5, 2.0)
    kv_weight = normal_values(key_list[4], (KVROWS, LATENT), NOPE ** -0.5, 0.5, ((0, 32),))
    kv_scales = jnp.clip(jnp.exp(math.log(2.0) - 1.3862944 * jax.random.uniform(key_list[5], (KVROWS // BLOCK, LATENT // BLOCK), jnp.float32) ** shard_levels(key_list[5], (KVROWS // BLOCK, LATENT // BLOCK), ((0, 4),), -0.2, 0.2)), 0.5, 2.0)
    kv_gain = jnp.clip(1.0 + 0.18 * jax.random.normal(key_list[6], (LATENT,), jnp.float32), 0.1, 1.9)
    pool_latent = draw_pool_latent(jax.random.fold_in(key_list[11], 71), 0)
    pool_rope = normal_values(key_list[8], (POOL, PAGE * ROPE), 1.0, 6.0, ((0, 8),))
    page_table = draw_page_table(jax.random.fold_in(key_list[11], 71), 0)
    prior_len = draw_prior_len(jax.random.fold_in(key_list[11], 71), 0)
    return dict(query_latent=query_latent, new_kv=new_kv, q_weight=q_weight, q_scales=q_scales, kv_weight=kv_weight, kv_scales=kv_scales, kv_gain=kv_gain, pool_latent=pool_latent, pool_rope=pool_rope, page_table=page_table, prior_len=prior_len)


NORM_EPS = 1e-06

def rope_tables(positions):
    half_width = ROPE // 2
    frequency = 10000.0 ** (-2.0 * jnp.arange(half_width, dtype=jnp.float32) / ROPE)
    angles = positions.astype(jnp.float32)[:, None] * frequency[None, :]
    return (jnp.cos(angles), jnp.sin(angles))

def rotate(values, cosine, sine_table):
    half_width = values.shape[-1] // 2
    leading = values[..., :half_width]
    trailing = values[..., half_width:]
    return jnp.concatenate([leading * cosine - trailing * sine_table, trailing * cosine + leading * sine_table], axis=-1)

def dequantize(values, scale_grid):
    expanded = jnp.repeat(jnp.repeat(scale_grid.astype(jnp.float32), BLOCK, axis=0), BLOCK, axis=1)
    return (values.astype(jnp.float32) * expanded).astype(jnp.bfloat16)

def reference(query_latent, new_kv, q_weight, q_scales, kv_weight, kv_scales, kv_gain, pool_latent, pool_rope, page_table, prior_len):
    query_weight = dequantize(q_weight, q_scales)
    kv_full = dequantize(kv_weight, kv_scales).reshape(HEADS, NOPE + VDIM, LATENT)
    key_weight = kv_full[:, :NOPE, :].astype(jnp.float32)
    value_weight = kv_full[:, NOPE:, :].astype(jnp.float32)
    score_scale = 1.0 / math.sqrt(NOPE + ROPE)
    prior_keys = PAGES * PAGE

    def one_reply(reply):
        first_row = reply * REPLY_TOK
        query_rows = lax.dynamic_slice_in_dim(query_latent, first_row, REPLY_TOK, 0)
        new_rows = lax.dynamic_slice_in_dim(new_kv, first_row, REPLY_TOK, 0)
        queries = jnp.dot(query_rows, query_weight, preferred_element_type=jnp.float32).astype(jnp.bfloat16)
        queries = queries.reshape(REPLY_TOK, HEADS, NOPE + ROPE)
        length = prior_len[reply]
        positions = length + jnp.arange(REPLY_TOK, dtype=jnp.int32)
        cosine, sine_table = rope_tables(positions)
        query_rope = rotate(queries[:, :, NOPE:].astype(jnp.float32), cosine[:, None, :], sine_table[:, None, :]).astype(jnp.bfloat16)
        query_lat = jnp.einsum('thd,hdc->thc', queries[:, :, :NOPE].astype(jnp.float32), key_weight).astype(jnp.bfloat16)
        latent_part = new_rows[:, :LATENT].astype(jnp.float32)
        inv_rms = lax.rsqrt(lax.optimization_barrier(jnp.mean(latent_part * latent_part, axis=-1, keepdims=True)) + NORM_EPS)
        new_lat = (latent_part * inv_rms * kv_gain.astype(jnp.float32)[None, :]).astype(jnp.bfloat16)
        new_rope = rotate(new_rows[:, LATENT:].astype(jnp.float32), cosine, sine_table).astype(jnp.bfloat16)
        table_row = page_table[reply]
        prior_lat = pool_latent[table_row].reshape(prior_keys, LATENT)
        prior_rope = pool_rope[table_row].reshape(prior_keys, ROPE)
        keys_lat = jnp.concatenate([prior_lat, new_lat], axis=0).astype(jnp.float32)
        keys_rope = jnp.concatenate([prior_rope, new_rope], axis=0).astype(jnp.float32)
        scores = jnp.einsum('thc,kc->htk', query_lat.astype(jnp.float32), keys_lat)
        scores = (scores + jnp.einsum('thr,kr->htk', query_rope.astype(jnp.float32), keys_rope)) * score_scale
        key_index = jnp.arange(prior_keys + REPLY_TOK, dtype=jnp.int32)[None, :]
        query_index = jnp.arange(REPLY_TOK, dtype=jnp.int32)[:, None]
        visible = jnp.where(key_index < prior_keys, key_index < length, key_index - prior_keys <= query_index)
        scores = jnp.where(visible[None], scores, -jnp.inf)
        row_max = lax.optimization_barrier(jnp.max(scores, axis=2, keepdims=True))
        exponent = jnp.exp(scores - row_max)
        weights = (exponent / lax.optimization_barrier(jnp.sum(exponent, axis=2, keepdims=True))).astype(jnp.bfloat16)
        mixed = jnp.einsum('htk,kc->thc', weights.astype(jnp.float32), keys_lat).astype(jnp.bfloat16)
        attended = jnp.einsum('thc,hvc->thv', mixed.astype(jnp.float32), value_weight).astype(jnp.bfloat16)
        return attended.reshape(REPLY_TOK, HEADS * VDIM)
    outputs = lax.map(one_reply, jnp.arange(REPLIES, dtype=jnp.int32))
    return outputs.reshape(REPLIES * REPLY_TOK, HEADS * VDIM)
```

```python
import functools
import math

import jax
import jax.numpy as jnp
from jax import lax
from jax.experimental import pallas as pl
from jax.experimental.pallas import tpu as pltpu
from jax.sharding import PartitionSpec as P

NOPE = 128
ROPE = 64
VDIM = 128
LATENT = 512
BLOCK = 128


NORM_EPS = 1e-06


def rope_tables(positions):
    half_width = ROPE // 2
    frequency = 10000.0 ** (-2.0 * jnp.arange(half_width, dtype=jnp.float32) / ROPE)
    angles = positions.astype(jnp.float32)[:, None] * frequency[None, :]
    return (jnp.cos(angles), jnp.sin(angles))


def rotate(values, cosine, sine_table):
    half_width = values.shape[-1] // 2
    leading = values[..., :half_width]
    trailing = values[..., half_width:]
    return jnp.concatenate(
        [leading * cosine - trailing * sine_table, trailing * cosine + leading * sine_table],
        axis=-1,
    )


def dequantize_rows(values, scale_grid, first_row):
    row_ids = (first_row + jnp.arange(values.shape[0], dtype=jnp.int32)) // BLOCK
    row_pick = (
        row_ids[:, None] == jnp.arange(scale_grid.shape[0], dtype=jnp.int32)[None, :]
    ).astype(jnp.float32)
    per_row = jnp.sum(row_pick[:, :, None] * scale_grid[None, :, :], axis=1)
    factors = jnp.repeat(per_row, BLOCK, axis=1)
    return (values.astype(jnp.float32) * factors).astype(jnp.bfloat16)


def add_rows(query_rows, weight_rows, offset, scale_grid):
    dense_rows = dequantize_rows(weight_rows, scale_grid, offset)
    return jnp.dot(query_rows, dense_rows, preferred_element_type=jnp.float32)


def body(
    query_latent,
    new_kv,
    q_weight,
    q_scales,
    kv_weight,
    kv_scales,
    kv_gain,
    pool_latent,
    pool_rope,
    page_table,
    prior_len,
):
    seq_count = lax.axis_size("seq")
    own_index = lax.axis_index("seq")
    query_rows, new_rows = (
        lax.all_gather(query_latent, "mp", axis=0, tiled=True),
        lax.all_gather(new_kv, "mp", axis=0, tiled=True),
    )
    tok_rows = query_rows.shape[0]
    q_full = add_rows(
        query_rows, lax.all_gather(q_weight, "seq", axis=0, tiled=True), jnp.int32(0), q_scales
    )
    kv_panel = lax.all_gather(kv_weight, "seq", axis=0, tiled=True)
    head_count = kv_panel.shape[0] // (NOPE + VDIM)
    kv_dense = dequantize_rows(kv_panel, kv_scales, 0).reshape(head_count, NOPE + VDIM, LATENT)
    key_weight = kv_dense[:, :NOPE, :]
    value_weight = kv_dense[:, NOPE:, :]
    queries = q_full.astype(jnp.bfloat16).reshape(tok_rows, head_count, NOPE + ROPE)
    length = lax.dynamic_index_in_dim(prior_len, own_index, 0, keepdims=False)
    positions = length + jnp.arange(tok_rows, dtype=jnp.int32)
    cosine, sine_table = rope_tables(positions)
    query_rope = rotate(
        queries[:, :, NOPE:].astype(jnp.float32), cosine[:, None, :], sine_table[:, None, :]
    ).astype(jnp.bfloat16)
    query_lat = jnp.einsum(
        "thd,hdc->thc", queries[:, :, :NOPE], key_weight, preferred_element_type=jnp.float32
    ).astype(jnp.bfloat16)
    latent_part = new_rows[:, :LATENT].astype(jnp.float32)
    inv_rms = lax.rsqrt(jnp.mean(latent_part * latent_part, axis=-1, keepdims=True) + NORM_EPS)
    new_lat = (latent_part * inv_rms * kv_gain[None, :]).astype(jnp.bfloat16)
    new_rope = rotate(new_rows[:, LATENT:].astype(jnp.float32), cosine, sine_table).astype(
        jnp.bfloat16
    )
    page_count = page_table.shape[1]
    pool_count = pool_latent.shape[0]
    page_len = pool_latent.shape[1]
    holders = page_table // pool_count
    pool_slots = page_table % pool_count
    earlier = jnp.arange(page_count)[None, :] < jnp.arange(page_count)[:, None]
    same_holder = holders[:, :, None] == holders[:, None, :]
    page_ranks = jnp.sum(jnp.where(same_holder & earlier[None], 1, 0), axis=2)
    capacity = (page_count + seq_count - 1) // seq_count
    wanted = (holders[:, None, :] == own_index) & (
        page_ranks[:, None, :] == jnp.arange(capacity)[None, :, None]
    )
    send_slot = jnp.sum(jnp.where(wanted, pool_slots[:, None, :], 0), axis=2).reshape(-1)
    send_lat = pool_latent[send_slot].reshape(seq_count, capacity, page_len, LATENT)
    send_rope = pool_rope[send_slot].reshape(seq_count, capacity, pool_rope.shape[1])
    got_lat, got_rope = (
        lax.all_to_all(send_lat, "seq", split_axis=0, concat_axis=0, tiled=True),
        lax.all_to_all(send_rope, "seq", split_axis=0, concat_axis=0, tiled=True),
    )
    own_holders = lax.dynamic_index_in_dim(holders, own_index, 0, keepdims=False)
    own_ranks = lax.dynamic_index_in_dim(page_ranks, own_index, 0, keepdims=False)
    where_from = own_holders * capacity + own_ranks
    prior_keys = page_count * page_len
    prior_lat = got_lat.reshape(seq_count * capacity, page_len, LATENT)[where_from].reshape(
        prior_keys, LATENT
    )
    prior_rope = got_rope.reshape(seq_count * capacity, pool_rope.shape[1])[where_from].reshape(
        prior_keys, ROPE
    )
    score_scale = 1.0 / math.sqrt(NOPE + ROPE)

    def score_keys(keys_lat, keys_rope):
        lat_part = jnp.einsum(
            "thc,kc->htk", query_lat, keys_lat, preferred_element_type=jnp.float32
        )
        rope_part = jnp.einsum(
            "thr,kr->htk", query_rope, keys_rope, preferred_element_type=jnp.float32
        )
        return (lat_part + rope_part) * score_scale

    prior_scores = score_keys(prior_lat, prior_rope)
    prior_index = jnp.arange(prior_keys, dtype=jnp.int32)
    prior_scores = jnp.where(prior_index[None, None, :] < length, prior_scores, -jnp.inf)
    new_scores = score_keys(new_lat, new_rope)
    causal = jnp.arange(tok_rows)[None, :] <= jnp.arange(tok_rows)[:, None]
    new_scores = jnp.where(causal[None], new_scores, -jnp.inf)
    scores = jnp.concatenate([prior_scores, new_scores], axis=2)
    row_max = jnp.max(scores, axis=2, keepdims=True)
    exponent = jnp.exp(scores - row_max)
    weights = (exponent / jnp.sum(exponent, axis=2, keepdims=True)).astype(jnp.bfloat16)
    keys_lat = jnp.concatenate([prior_lat, new_lat], axis=0)
    mixed = jnp.einsum("htk,kc->thc", weights, keys_lat, preferred_element_type=jnp.float32).astype(
        jnp.bfloat16
    )
    attended = jnp.einsum(
        "thc,hvc->thv", mixed, value_weight, preferred_element_type=jnp.float32
    ).astype(jnp.bfloat16)
    return attended.reshape(tok_rows, head_count * VDIM)


MESH = pl.DeviceIdType.MESH
KEYW = LATENT + 2 * ROPE
HEADW = NOPE + ROPE
KV_UNITS = 4
Q_UNITS = 8
UNITS = KV_UNITS + Q_UNITS
LANES = 9
AHEAD = 3


def fused_kernel(
    query_ref,
    new_ref,
    pages_ref,
    qw_ref,
    kv_ref,
    qs_ref,
    ks_ref,
    cos_ref,
    sin_ref,
    bias_ref,
    out_ref,
    q_all,
    kv_all,
    keys,
    queries,
    wq,
    send_sem,
    recv_sem,
    page_send,
    page_recv,
    row_send,
    row_recv,
    own_sem,
):
    me = lax.axis_index("seq")
    z = lax.axis_index("mp")
    n_seq = pages_ref.shape[0]
    n_mp = queries.shape[0] // query_ref.shape[0]
    core = lax.rem(me, 2)
    across = lax.rem(me // 2, 2)
    down = me // 4
    sib = me + 1 - 2 * core
    xn = me + 2 - 4 * across
    yn = me + 4 - 8 * down
    dn = xn + 4 - 8 * down
    sib_x = sib + 2 - 4 * across
    sib_y = sib + 4 - 8 * down
    sib_d = sib_x + 4 - 8 * down

    q_rows = qw_ref.shape[0]
    q_cols = qw_ref.shape[1] // Q_UNITS
    kv_rows = kv_ref.shape[0]
    kv_part = kv_rows // KV_UNITS
    page_rows = pages_ref.shape[1]
    prior = n_seq * page_rows
    own_rows = query_ref.shape[0]
    toks = queries.shape[0]

    barrier = pltpu.get_barrier_semaphore()
    for i in range(1, n_seq):
        pl.semaphore_signal(
            barrier, inc=1, device_id=(lax.rem(me + i, n_seq), z), device_id_type=MESH
        )
    for i in range(1, n_mp):
        pl.semaphore_signal(
            barrier, inc=1, device_id=(me, lax.rem(z + i, n_mp)), device_id_type=MESH
        )
    pl.semaphore_wait(barrier, n_seq + n_mp - 2)

    def row_copies(i):
        target = (me, lax.rem(z + i, n_mp))
        return (
            pltpu.make_async_remote_copy(
                src_ref=query_ref,
                dst_ref=queries.at[pl.ds(z * own_rows, own_rows)],
                send_sem=row_send.at[2 * i],
                recv_sem=row_recv.at[2 * i],
                device_id=target,
                device_id_type=MESH,
            ),
            pltpu.make_async_remote_copy(
                src_ref=new_ref,
                dst_ref=keys.at[pl.ds(prior + z * own_rows, own_rows)],
                send_sem=row_send.at[2 * i + 1],
                recv_sem=row_recv.at[2 * i + 1],
                device_id=target,
                device_id_type=MESH,
            ),
        )

    def page_copy(i):
        target = lax.rem(me + i, n_seq)
        return pltpu.make_async_remote_copy(
            src_ref=pages_ref.at[target],
            dst_ref=keys.at[pl.ds(me * page_rows, page_rows)],
            send_sem=page_send.at[i],
            recv_sem=page_recv.at[i],
            device_id=(target, z),
            device_id_type=MESH,
        )

    def row_arrivals(i):
        owner = lax.rem(z + n_mp - i, n_mp)
        for kind, (buf, base) in enumerate(((queries, 0), (keys, prior))):
            ref = buf.at[pl.ds(base + owner * own_rows, own_rows)]
            pltpu.make_async_remote_copy(
                src_ref=ref,
                dst_ref=ref,
                send_sem=row_send.at[2 * i + kind],
                recv_sem=row_recv.at[2 * i + kind],
                device_id=(me, owner),
                device_id_type=MESH,
            ).wait_recv()

    def page_arrival(i):
        owner = lax.rem(me + n_seq - i, n_seq)
        ref = keys.at[pl.ds(owner * page_rows, page_rows)]
        pltpu.make_async_remote_copy(
            src_ref=ref,
            dst_ref=ref,
            send_sem=page_send.at[i],
            recv_sem=page_recv.at[i],
            device_id=(owner, z),
            device_id_type=MESH,
        ).wait_recv()

    local = [
        pltpu.make_async_copy(
            query_ref, queries.at[pl.ds(z * own_rows, own_rows)], own_sem.at[Q_UNITS]
        ),
        pltpu.make_async_copy(
            new_ref, keys.at[pl.ds(prior + z * own_rows, own_rows)], own_sem.at[Q_UNITS + 1]
        ),
        pltpu.make_async_copy(
            pages_ref.at[me], keys.at[pl.ds(me * page_rows, page_rows)], own_sem.at[Q_UNITS + 2]
        ),
        pltpu.make_async_copy(
            kv_ref, kv_all.at[pl.ds(me * kv_rows, kv_rows)], own_sem.at[Q_UNITS + 3]
        ),
    ]

    def own_panel(k):
        return pltpu.make_async_copy(
            qw_ref.at[:, pl.ds(pl.multiple_of(k * q_cols, 128), q_cols)],
            q_all.at[k, pl.ds(me * q_rows, q_rows)],
            own_sem.at[k],
        )

    def place(is_q, owner, unit, half):
        if is_q:
            step = q_rows // 2
            start, size = (owner * q_rows, q_rows) if half is None else (
                owner * q_rows + half * step, step)
            return q_all.at[unit - KV_UNITS, pl.ds(start, size)]
        step = kv_part // 2
        base = owner * kv_rows + unit * kv_part
        start, size = (base, kv_part) if half is None else (base + half * step, step)
        return kv_all.at[pl.ds(start, size)]

    def own_source(is_q, unit):
        if is_q:
            first = pl.multiple_of((unit - KV_UNITS) * q_cols, 128)
            return qw_ref.at[:, pl.ds(first, q_cols)]
        return kv_ref.at[pl.ds(unit * kv_part, kv_part)]

    def link(src, dst, unit, lane, target):
        at = unit * LANES + lane
        return pltpu.make_async_remote_copy(
            src_ref=src,
            dst_ref=dst,
            send_sem=send_sem.at[at],
            recv_sem=recv_sem.at[at],
            device_id=(target, z),
            device_id_type=MESH,
        )

    def arrived(is_q, unit, lane, owner, half, sender):
        ref = place(is_q, owner, unit, half)
        link(ref, ref, unit, lane, sender).wait_recv()

    def forward(is_q, unit, lane, owner, half, target):
        ref = place(is_q, owner, unit, half)
        link(ref, ref, unit, lane, target).start()

    def each_kind(low, high, unit, act):
        @pl.when((unit >= low) & (unit < KV_UNITS))
        def _():
            act(False)

        @pl.when((unit >= KV_UNITS) & (unit < high))
        def _():
            act(True)

    def send_own(unit):
        def act(is_q):
            src = own_source(is_q, unit)
            dst = place(is_q, me, unit, None)
            link(src, dst, unit, 0, xn).start()
            link(src, dst, unit, 1, yn).start()
            link(src, dst, unit, 4, sib).start()

        each_kind(0, UNITS, unit, act)

    def relay(unit):
        def act(is_q):
            arrived(is_q, unit, 0, xn, None, xn)
            forward(is_q, unit, 2, xn, 0, yn)
            forward(is_q, unit, 5, xn, None, sib)
            arrived(is_q, unit, 1, yn, None, yn)
            forward(is_q, unit, 3, yn, 1, xn)
            forward(is_q, unit, 6, yn, None, sib)

        each_kind(0, UNITS, unit, act)

    def share(unit):
        def act(is_q):
            arrived(is_q, unit, 2, dn, 0, yn)
            forward(is_q, unit, 7, dn, 0, sib)
            arrived(is_q, unit, 3, dn, 1, xn)
            forward(is_q, unit, 8, dn, 1, sib)

        each_kind(0, UNITS, unit, act)

    def collect(unit):
        def act(is_q):
            arrived(is_q, unit, 4, sib, None, sib)
            arrived(is_q, unit, 5, sib_x, None, sib)
            arrived(is_q, unit, 6, sib_y, None, sib)
            arrived(is_q, unit, 7, sib_d, 0, sib)
            arrived(is_q, unit, 8, sib_d, 1, sib)

        each_kind(0, UNITS, unit, act)

    def sent(unit):
        def act(is_q):
            whole = place(is_q, me, unit, None)
            part = place(is_q, me, unit, 0)
            for lane in (0, 1, 4, 5, 6):
                link(whole, whole, unit, lane, sib).wait_send()
            for lane in (2, 3, 7, 8):
                link(part, part, unit, lane, sib).wait_send()

        each_kind(0, UNITS, unit, act)

    lane_id = lax.broadcasted_iota(jnp.int32, (toks, 2 * ROPE), 1)
    low_half = lane_id < ROPE
    low_quarter = lax.rem(lane_id, ROPE) < ROPE // 2
    scale = math.log2(math.e) / math.sqrt(NOPE + ROPE)

    def scale_row(ref, row, first, count):
        return jnp.concatenate(
            [jnp.full((1, BLOCK), ref[row, first + b], jnp.float32) for b in range(count)], axis=1
        )

    def two_heads(pair, unit, side):
        for b in range(wq.shape[0] // BLOCK):
            rows = slice(b * BLOCK, (b + 1) * BLOCK)
            block = q_all[unit, rows, side * 2 * HEADW : (side + 1) * 2 * HEADW]
            wq[rows, :] = (
                block.astype(jnp.float32) * scale_row(qs_ref, b, 3 * pair, 3)
            ).astype(jnp.bfloat16)
        q = jnp.dot(queries[...], wq[...], preferred_element_type=jnp.float32)
        q = q.astype(jnp.bfloat16).astype(jnp.float32)
        mid, end = q[:, NOPE : 2 * NOPE], q[:, 2 * NOPE :]
        nope = (
            q[:, :NOPE].astype(jnp.bfloat16),
            jnp.where(low_half, pltpu.roll(mid, ROPE, 1), pltpu.roll(end, ROPE, 1)).astype(
                jnp.bfloat16
            ),
        )
        flat = jnp.where(low_half, mid, end)
        swapped = jnp.where(low_quarter, pltpu.roll(flat, 96, 1), pltpu.roll(flat, 32, 1))
        turned = flat * cos_ref[...] + swapped * sin_ref[...]
        ropes = (turned.astype(jnp.bfloat16), pltpu.roll(turned, ROPE, 1).astype(jnp.bfloat16))
        row_id = lax.broadcasted_iota(jnp.int32, (toks, toks), 0)
        col_id = lax.broadcasted_iota(jnp.int32, (toks, toks), 1)
        causal = col_id <= row_id
        outs = []
        for side_head in range(2):
            head = 2 * pair + side_head
            first = pl.multiple_of(head * 2 * BLOCK, 2 * BLOCK)
            wk = (
                kv_all[pl.ds(first, BLOCK), :].astype(jnp.float32)
                * scale_row(ks_ref, 2 * head, 0, LATENT // BLOCK)
            ).astype(jnp.bfloat16)
            wv = (
                kv_all[pl.ds(first + BLOCK, BLOCK), :].astype(jnp.float32)
                * scale_row(ks_ref, 2 * head + 1, 0, LATENT // BLOCK)
            ).astype(jnp.bfloat16)
            lat = jnp.dot(nope[side_head], wk, preferred_element_type=jnp.float32).astype(
                jnp.bfloat16
            )
            full = jnp.concatenate([lat, ropes[side_head]], axis=1)
            dims = (((1,), (1,)), ((), ()))
            s = lax.dot_general(full, keys[...], dims, preferred_element_type=jnp.float32)
            s_old = s[:, :prior] + bias_ref[...]
            s_new = jnp.where(causal, s[:, prior:], -jnp.inf)
            s = jnp.concatenate([s_old, s_new], axis=1)
            top = jnp.max(s, axis=1, keepdims=True)
            e = jnp.exp2((s - top) * scale)
            w = (e * (1.0 / jnp.sum(e, axis=1, keepdims=True))).astype(jnp.bfloat16)
            mixed = jnp.dot(w, keys[:, :LATENT], preferred_element_type=jnp.float32).astype(
                jnp.bfloat16
            )
            outs.append(
                lax.dot_general(mixed, wv, dims, preferred_element_type=jnp.float32).astype(
                    jnp.bfloat16
                )
            )
        out_ref[:, pl.ds(pl.multiple_of(pair * 2 * VDIM, 2 * VDIM), 2 * VDIM)] = jnp.concatenate(
            outs, axis=1
        )

    for i in range(1, n_mp):
        for copy in row_copies(i):
            copy.start()
    for i in range(1, n_seq):
        page_copy(i).start()
    for u in range(AHEAD):
        send_own(jnp.int32(u))
    for copy in local:
        copy.start()
    for k in range(Q_UNITS):
        own_panel(k).start()

    def step(t, carry):
        relay(t)
        send_own(t + AHEAD)
        share(t - 1)
        collect(t - 2)

        @pl.when(t - 2 == KV_UNITS)
        def _():
            for i in range(1, n_mp):
                row_arrivals(i)
            for i in range(1, n_seq):
                page_arrival(i)
            for copy in local:
                copy.wait()

        @pl.when(t - 2 >= KV_UNITS)
        def _():
            k = t - 2 - KV_UNITS
            own_panel(k).wait()
            two_heads(2 * k, k, 0)
            two_heads(2 * k + 1, k, 1)

        return carry

    lax.fori_loop(0, UNITS + 2, step, 0)

    for i in range(1, n_mp):
        for copy in row_copies(i):
            copy.wait_send()
    for i in range(1, n_seq):
        page_copy(i).wait_send()

    def drain(u, carry):
        sent(u)
        return carry

    lax.fori_loop(0, UNITS, drain, 0)


def fused_body(
    query_latent,
    new_kv,
    q_weight,
    q_scales,
    kv_weight,
    kv_scales,
    kv_gain,
    pool_latent,
    pool_rope,
    page_table,
    prior_len,
):
    seq_count = lax.axis_size("seq")
    mp_count = lax.axis_size("mp")
    own_index = lax.axis_index("seq")
    mp_index = lax.axis_index("mp")
    own_rows = query_latent.shape[0]
    toks = own_rows * mp_count
    page_count = page_table.shape[1]
    pool_count, page_len = pool_latent.shape[:2]
    length = lax.dynamic_index_in_dim(prior_len, own_index, 0, keepdims=False)
    cosine, sine = rope_tables(length + jnp.arange(toks, dtype=jnp.int32))
    cos_table = jnp.tile(cosine, (1, 4))
    sin_table = jnp.tile(jnp.concatenate([-sine, sine], axis=1), (1, 2))

    first = mp_index * own_rows
    own_cos = lax.dynamic_slice_in_dim(cosine, first, own_rows, 0)
    own_sin = lax.dynamic_slice_in_dim(sine, first, own_rows, 0)
    latent_part = new_kv[:, :LATENT].astype(jnp.float32)
    inv_rms = lax.rsqrt(jnp.mean(latent_part * latent_part, axis=-1, keepdims=True) + NORM_EPS)
    new_lat = latent_part * inv_rms * kv_gain[None, :]
    new_rope = rotate(new_kv[:, LATENT:].astype(jnp.float32), own_cos, own_sin)
    new_keys = jnp.concatenate([new_lat, new_rope, jnp.zeros_like(new_rope)], axis=1).astype(
        jnp.bfloat16
    )

    holders = page_table // pool_count
    pool_slots = page_table % pool_count
    earlier = jnp.arange(page_count)[None, :] < jnp.arange(page_count)[:, None]
    same_holder = holders[:, :, None] == holders[:, None, :]
    page_ranks = jnp.sum(jnp.where(same_holder & earlier[None], 1, 0), axis=2)
    capacity = (page_count + seq_count - 1) // seq_count
    wanted = (holders[:, None, :] == own_index) & (
        page_ranks[:, None, :] == jnp.arange(capacity)[None, :, None]
    )
    send_slot = jnp.sum(jnp.where(wanted, pool_slots[:, None, :], 0), axis=2).reshape(-1)
    rope_rows = pool_rope.reshape(pool_count, page_len, ROPE)
    pool_keys = jnp.concatenate([pool_latent, rope_rows, jnp.zeros_like(rope_rows)], axis=2)
    pages = pool_keys[send_slot].reshape(seq_count, capacity * page_len, KEYW)

    own_place = lax.dynamic_index_in_dim(holders * capacity + page_ranks, own_index, 0, False)
    at_slot = own_place[None, :] == jnp.arange(seq_count * capacity)[:, None]
    slot_page = jnp.sum(jnp.where(at_slot, jnp.arange(page_count)[None, :], 0), axis=1)
    slot_page = jnp.where(jnp.any(at_slot, axis=1), slot_page, page_count)
    token = slot_page[:, None] * page_len + jnp.arange(page_len)[None, :]
    seen = token < jnp.minimum(length, page_count * page_len)
    bias = jnp.where(seen, 0.0, -jnp.inf).astype(jnp.float32).reshape(1, -1)

    prior = seq_count * capacity * page_len
    heads = q_weight.shape[1] // HEADW
    anywhere = pl.BlockSpec(memory_space=pl.ANY)
    vmem = pl.BlockSpec(memory_space=pltpu.VMEM)
    smem = pl.BlockSpec(memory_space=pltpu.SMEM)
    return pl.pallas_call(
        fused_kernel,
        out_shape=jax.ShapeDtypeStruct((toks, heads * VDIM), jnp.bfloat16),
        in_specs=[anywhere] * 5 + [smem] * 2 + [vmem] * 3,
        out_specs=vmem,
        scratch_shapes=[
            pltpu.VMEM(
                (Q_UNITS, q_weight.shape[0] * seq_count, q_weight.shape[1] // Q_UNITS),
                jnp.bfloat16,
            ),
            pltpu.VMEM((kv_weight.shape[0] * seq_count, LATENT), jnp.bfloat16),
            pltpu.VMEM((prior + toks, KEYW), jnp.bfloat16),
            pltpu.VMEM((toks, query_latent.shape[1]), jnp.bfloat16),
            pltpu.VMEM((q_weight.shape[0] * seq_count, 2 * HEADW), jnp.bfloat16),
            pltpu.SemaphoreType.DMA((UNITS * LANES,)),
            pltpu.SemaphoreType.DMA((UNITS * LANES,)),
            pltpu.SemaphoreType.DMA((seq_count,)),
            pltpu.SemaphoreType.DMA((seq_count,)),
            pltpu.SemaphoreType.DMA((2 * mp_count,)),
            pltpu.SemaphoreType.DMA((2 * mp_count,)),
            pltpu.SemaphoreType.DMA((Q_UNITS + 4,)),
        ],
        compiler_params=pltpu.CompilerParams(
            collective_id=0, has_side_effects=True, vmem_limit_bytes=56 * 1024 * 1024
        ),
        cost_estimate=pl.CostEstimate(
            flops=30 * 10**9, bytes_accessed=10**7, transcendentals=10**7
        ),
    )(
        query_latent,
        new_keys,
        pages,
        q_weight,
        kv_weight,
        q_scales,
        kv_scales,
        cos_table,
        sin_table,
        bias,
    )


def solution(mesh):
    in_specs = (
        P(("seq", "mp"), None),
        P(("seq", "mp"), None),
        P("seq", "mp"),
        P(None, "mp"),
        P(("mp", "seq"), None),
        P("mp", None),
        P(),
        P("seq", None, None),
        P("seq", None),
        P(),
        P(),
    )
    out_specs = P("seq", "mp")
    fused = mesh.shape["seq"] == 8 and mesh.shape["mp"] == 4
    return jax.shard_map(
        fused_body if fused else body,
        mesh=mesh,
        in_specs=in_specs,
        out_specs=out_specs,
        check_vma=False,
    )
```

```python
import functools
import math

import jax
import jax.numpy as jnp
from jax import lax
from jax.experimental import pallas as pl
from jax.experimental.pallas import tpu as pltpu
from jax.sharding import PartitionSpec as P

NOPE = 128
ROPE = 64
VDIM = 128
LATENT = 512
BLOCK = 128


NORM_EPS = 1e-06


def rope_tables(positions):
    half_width = ROPE // 2
    frequency = 10000.0 ** (-2.0 * jnp.arange(half_width, dtype=jnp.float32) / ROPE)
    angles = positions.astype(jnp.float32)[:, None] * frequency[None, :]
    return (jnp.cos(angles), jnp.sin(angles))


def rotate(values, cosine, sine_table):
    half_width = values.shape[-1] // 2
    leading = values[..., :half_width]
    trailing = values[..., half_width:]
    return jnp.concatenate(
        [leading * cosine - trailing * sine_table, trailing * cosine + leading * sine_table],
        axis=-1,
    )


def dequantize_rows(values, scale_grid, first_row):
    row_ids = (first_row + jnp.arange(values.shape[0], dtype=jnp.int32)) // BLOCK
    row_pick = (
        row_ids[:, None] == jnp.arange(scale_grid.shape[0], dtype=jnp.int32)[None, :]
    ).astype(jnp.float32)
    per_row = jnp.sum(row_pick[:, :, None] * scale_grid[None, :, :], axis=1)
    factors = jnp.repeat(per_row, BLOCK, axis=1)
    return (values.astype(jnp.float32) * factors).astype(jnp.bfloat16)


def add_rows(query_rows, weight_rows, offset, scale_grid):
    dense_rows = dequantize_rows(weight_rows, scale_grid, offset)
    return jnp.dot(query_rows, dense_rows, preferred_element_type=jnp.float32)


def body(
    query_latent,
    new_kv,
    q_weight,
    q_scales,
    kv_weight,
    kv_scales,
    kv_gain,
    pool_latent,
    pool_rope,
    page_table,
    prior_len,
):
    seq_count = lax.axis_size("seq")
    own_index = lax.axis_index("seq")
    query_rows, new_rows = (
        lax.all_gather(query_latent, "mp", axis=0, tiled=True),
        lax.all_gather(new_kv, "mp", axis=0, tiled=True),
    )
    tok_rows = query_rows.shape[0]
    q_full = add_rows(
        query_rows, lax.all_gather(q_weight, "seq", axis=0, tiled=True), jnp.int32(0), q_scales
    )
    kv_panel = lax.all_gather(kv_weight, "seq", axis=0, tiled=True)
    head_count = kv_panel.shape[0] // (NOPE + VDIM)
    kv_dense = dequantize_rows(kv_panel, kv_scales, 0).reshape(head_count, NOPE + VDIM, LATENT)
    key_weight = kv_dense[:, :NOPE, :]
    value_weight = kv_dense[:, NOPE:, :]
    queries = q_full.astype(jnp.bfloat16).reshape(tok_rows, head_count, NOPE + ROPE)
    length = lax.dynamic_index_in_dim(prior_len, own_index, 0, keepdims=False)
    positions = length + jnp.arange(tok_rows, dtype=jnp.int32)
    cosine, sine_table = rope_tables(positions)
    query_rope = rotate(
        queries[:, :, NOPE:].astype(jnp.float32), cosine[:, None, :], sine_table[:, None, :]
    ).astype(jnp.bfloat16)
    query_lat = jnp.einsum(
        "thd,hdc->thc", queries[:, :, :NOPE], key_weight, preferred_element_type=jnp.float32
    ).astype(jnp.bfloat16)
    latent_part = new_rows[:, :LATENT].astype(jnp.float32)
    inv_rms = lax.rsqrt(jnp.mean(latent_part * latent_part, axis=-1, keepdims=True) + NORM_EPS)
    new_lat = (latent_part * inv_rms * kv_gain[None, :]).astype(jnp.bfloat16)
    new_rope = rotate(new_rows[:, LATENT:].astype(jnp.float32), cosine, sine_table).astype(
        jnp.bfloat16
    )
    page_count = page_table.shape[1]
    pool_count = pool_latent.shape[0]
    page_len = pool_latent.shape[1]
    holders = page_table // pool_count
    pool_slots = page_table % pool_count
    earlier = jnp.arange(page_count)[None, :] < jnp.arange(page_count)[:, None]
    same_holder = holders[:, :, None] == holders[:, None, :]
    page_ranks = jnp.sum(jnp.where(same_holder & earlier[None], 1, 0), axis=2)
    capacity = (page_count + seq_count - 1) // seq_count
    wanted = (holders[:, None, :] == own_index) & (
        page_ranks[:, None, :] == jnp.arange(capacity)[None, :, None]
    )
    send_slot = jnp.sum(jnp.where(wanted, pool_slots[:, None, :], 0), axis=2).reshape(-1)
    send_lat = pool_latent[send_slot].reshape(seq_count, capacity, page_len, LATENT)
    send_rope = pool_rope[send_slot].reshape(seq_count, capacity, pool_rope.shape[1])
    got_lat, got_rope = (
        lax.all_to_all(send_lat, "seq", split_axis=0, concat_axis=0, tiled=True),
        lax.all_to_all(send_rope, "seq", split_axis=0, concat_axis=0, tiled=True),
    )
    own_holders = lax.dynamic_index_in_dim(holders, own_index, 0, keepdims=False)
    own_ranks = lax.dynamic_index_in_dim(page_ranks, own_index, 0, keepdims=False)
    where_from = own_holders * capacity + own_ranks
    prior_keys = page_count * page_len
    prior_lat = got_lat.reshape(seq_count * capacity, page_len, LATENT)[where_from].reshape(
        prior_keys, LATENT
    )
    prior_rope = got_rope.reshape(seq_count * capacity, pool_rope.shape[1])[where_from].reshape(
        prior_keys, ROPE
    )
    score_scale = 1.0 / math.sqrt(NOPE + ROPE)

    def score_keys(keys_lat, keys_rope):
        lat_part = jnp.einsum(
            "thc,kc->htk", query_lat, keys_lat, preferred_element_type=jnp.float32
        )
        rope_part = jnp.einsum(
            "thr,kr->htk", query_rope, keys_rope, preferred_element_type=jnp.float32
        )
        return (lat_part + rope_part) * score_scale

    prior_scores = score_keys(prior_lat, prior_rope)
    prior_index = jnp.arange(prior_keys, dtype=jnp.int32)
    prior_scores = jnp.where(prior_index[None, None, :] < length, prior_scores, -jnp.inf)
    new_scores = score_keys(new_lat, new_rope)
    causal = jnp.arange(tok_rows)[None, :] <= jnp.arange(tok_rows)[:, None]
    new_scores = jnp.where(causal[None], new_scores, -jnp.inf)
    scores = jnp.concatenate([prior_scores, new_scores], axis=2)
    row_max = jnp.max(scores, axis=2, keepdims=True)
    exponent = jnp.exp(scores - row_max)
    weights = (exponent / jnp.sum(exponent, axis=2, keepdims=True)).astype(jnp.bfloat16)
    keys_lat = jnp.concatenate([prior_lat, new_lat], axis=0)
    mixed = jnp.einsum("htk,kc->thc", weights, keys_lat, preferred_element_type=jnp.float32).astype(
        jnp.bfloat16
    )
    attended = jnp.einsum(
        "thc,hvc->thv", mixed, value_weight, preferred_element_type=jnp.float32
    ).astype(jnp.bfloat16)
    return attended.reshape(tok_rows, head_count * VDIM)


MESH = pl.DeviceIdType.MESH
KEYW = LATENT + 2 * ROPE
HEADW = NOPE + ROPE
KV_UNITS = 4
Q_UNITS = 8
UNITS = KV_UNITS + Q_UNITS
LANES = 9
AHEAD = 3


def fused_kernel(
    query_ref,
    new_ref,
    pages_ref,
    qw_ref,
    kv_ref,
    qs_ref,
    ks_ref,
    cos_ref,
    sin_ref,
    bias_ref,
    out_ref,
    q_all,
    kv_all,
    keys,
    queries,
    wq,
    send_sem,
    recv_sem,
    page_send,
    page_recv,
    row_send,
    row_recv,
    own_sem,
):
    me = lax.axis_index("seq")
    z = lax.axis_index("mp")
    n_seq = pages_ref.shape[0]
    n_mp = queries.shape[0] // query_ref.shape[0]
    core = lax.rem(me, 2)
    across = lax.rem(me // 2, 2)
    down = me // 4
    sib = me + 1 - 2 * core
    xn = me + 2 - 4 * across
    yn = me + 4 - 8 * down
    dn = xn + 4 - 8 * down
    sib_x = sib + 2 - 4 * across
    sib_y = sib + 4 - 8 * down
    sib_d = sib_x + 4 - 8 * down

    q_rows = qw_ref.shape[0]
    q_cols = qw_ref.shape[1] // Q_UNITS
    kv_rows = kv_ref.shape[0]
    kv_part = kv_rows // KV_UNITS
    page_rows = pages_ref.shape[1]
    prior = n_seq * page_rows
    own_rows = query_ref.shape[0]
    toks = queries.shape[0]

    barrier = pltpu.get_barrier_semaphore()
    for i in range(1, n_seq):
        pl.semaphore_signal(
            barrier, inc=1, device_id=(lax.rem(me + i, n_seq), z), device_id_type=MESH
        )
    for i in range(1, n_mp):
        pl.semaphore_signal(
            barrier, inc=1, device_id=(me, lax.rem(z + i, n_mp)), device_id_type=MESH
        )
    pl.semaphore_wait(barrier, n_seq + n_mp - 2)

    def row_copies(i):
        target = (me, lax.rem(z + i, n_mp))
        return (
            pltpu.make_async_remote_copy(
                src_ref=query_ref,
                dst_ref=queries.at[pl.ds(z * own_rows, own_rows)],
                send_sem=row_send.at[2 * i],
                recv_sem=row_recv.at[2 * i],
                device_id=target,
                device_id_type=MESH,
            ),
            pltpu.make_async_remote_copy(
                src_ref=new_ref,
                dst_ref=keys.at[pl.ds(prior + z * own_rows, own_rows)],
                send_sem=row_send.at[2 * i + 1],
                recv_sem=row_recv.at[2 * i + 1],
                device_id=target,
                device_id_type=MESH,
            ),
        )

    def page_copy(i):
        target = lax.rem(me + i, n_seq)
        return pltpu.make_async_remote_copy(
            src_ref=pages_ref.at[target],
            dst_ref=keys.at[pl.ds(me * page_rows, page_rows)],
            send_sem=page_send.at[i],
            recv_sem=page_recv.at[i],
            device_id=(target, z),
            device_id_type=MESH,
        )

    def row_arrivals(i):
        owner = lax.rem(z + n_mp - i, n_mp)
        for kind, (buf, base) in enumerate(((queries, 0), (keys, prior))):
            ref = buf.at[pl.ds(base + owner * own_rows, own_rows)]
            pltpu.make_async_remote_copy(
                src_ref=ref,
                dst_ref=ref,
                send_sem=row_send.at[2 * i + kind],
                recv_sem=row_recv.at[2 * i + kind],
                device_id=(me, owner),
                device_id_type=MESH,
            ).wait_recv()

    def page_arrival(i):
        owner = lax.rem(me + n_seq - i, n_seq)
        ref = keys.at[pl.ds(owner * page_rows, page_rows)]
        pltpu.make_async_remote_copy(
            src_ref=ref,
            dst_ref=ref,
            send_sem=page_send.at[i],
            recv_sem=page_recv.at[i],
            device_id=(owner, z),
            device_id_type=MESH,
        ).wait_recv()

    local = [
        pltpu.make_async_copy(
            query_ref, queries.at[pl.ds(z * own_rows, own_rows)], own_sem.at[Q_UNITS]
        ),
        pltpu.make_async_copy(
            new_ref, keys.at[pl.ds(prior + z * own_rows, own_rows)], own_sem.at[Q_UNITS + 1]
        ),
        pltpu.make_async_copy(
            pages_ref.at[me], keys.at[pl.ds(me * page_rows, page_rows)], own_sem.at[Q_UNITS + 2]
        ),
        pltpu.make_async_copy(
            kv_ref, kv_all.at[pl.ds(me * kv_rows, kv_rows)], own_sem.at[Q_UNITS + 3]
        ),
    ]

    def own_panel(k):
        return pltpu.make_async_copy(
            qw_ref.at[:, pl.ds(pl.multiple_of(k * q_cols, 128), q_cols)],
            q_all.at[k, pl.ds(me * q_rows, q_rows)],
            own_sem.at[k],
        )

    def place(is_q, owner, unit, half):
        if is_q:
            step = q_rows // 2
            start, size = (owner * q_rows, q_rows) if half is None else (
                owner * q_rows + half * step, step)
            return q_all.at[unit - KV_UNITS, pl.ds(start, size)]
        step = kv_part // 2
        base = owner * kv_rows + unit * kv_part
        start, size = (base, kv_part) if half is None else (base + half * step, step)
        return kv_all.at[pl.ds(start, size)]

    def own_source(is_q, unit):
        if is_q:
            first = pl.multiple_of((unit - KV_UNITS) * q_cols, 128)
            return qw_ref.at[:, pl.ds(first, q_cols)]
        return kv_ref.at[pl.ds(unit * kv_part, kv_part)]

    def link(src, dst, unit, lane, target):
        at = unit * LANES + lane
        return pltpu.make_async_remote_copy(
            src_ref=src,
            dst_ref=dst,
            send_sem=send_sem.at[at],
            recv_sem=recv_sem.at[at],
            device_id=(target, z),
            device_id_type=MESH,
        )

    def arrived(is_q, unit, lane, owner, half, sender):
        ref = place(is_q, owner, unit, half)
        link(ref, ref, unit, lane, sender).wait_recv()

    def forward(is_q, unit, lane, owner, half, target):
        ref = place(is_q, owner, unit, half)
        link(ref, ref, unit, lane, target).start()

    def each_kind(low, high, unit, act):
        @pl.when((unit >= low) & (unit < KV_UNITS))
        def _():
            act(False)

        @pl.when((unit >= KV_UNITS) & (unit < high))
        def _():
            act(True)

    def send_own(unit):
        def act(is_q):
            src = own_source(is_q, unit)
            dst = place(is_q, me, unit, None)
            link(src, dst, unit, 0, xn).start()
            link(src, dst, unit, 1, yn).start()
            link(src, dst, unit, 4, sib).start()

        each_kind(0, UNITS, unit, act)

    def relay(unit):
        def act(is_q):
            arrived(is_q, unit, 0, xn, None, xn)
            forward(is_q, unit, 2, xn, 0, yn)
            forward(is_q, unit, 5, xn, None, sib)
            arrived(is_q, unit, 1, yn, None, yn)
            forward(is_q, unit, 3, yn, 1, xn)
            forward(is_q, unit, 6, yn, None, sib)

        each_kind(0, UNITS, unit, act)

    def share(unit):
        def act(is_q):
            arrived(is_q, unit, 2, dn, 0, yn)
            forward(is_q, unit, 7, dn, 0, sib)
            arrived(is_q, unit, 3, dn, 1, xn)
            forward(is_q, unit, 8, dn, 1, sib)

        each_kind(0, UNITS, unit, act)

    def collect(unit):
        def act(is_q):
            arrived(is_q, unit, 4, sib, None, sib)
            arrived(is_q, unit, 5, sib_x, None, sib)
            arrived(is_q, unit, 6, sib_y, None, sib)
            arrived(is_q, unit, 7, sib_d, 0, sib)
            arrived(is_q, unit, 8, sib_d, 1, sib)

        each_kind(0, UNITS, unit, act)

    def sent(unit):
        def act(is_q):
            whole = place(is_q, me, unit, None)
            part = place(is_q, me, unit, 0)
            for lane in (0, 1, 4, 5, 6):
                link(whole, whole, unit, lane, sib).wait_send()
            for lane in (2, 3, 7, 8):
                link(part, part, unit, lane, sib).wait_send()

        each_kind(0, UNITS, unit, act)

    lane_id = lax.broadcasted_iota(jnp.int32, (toks, 2 * ROPE), 1)
    low_half = lane_id < ROPE
    low_quarter = lax.rem(lane_id, ROPE) < ROPE // 2
    scale = math.log2(math.e) / math.sqrt(NOPE + ROPE)

    def scale_row(ref, row, first, count):
        return jnp.concatenate(
            [jnp.full((1, BLOCK), ref[row, first + b], jnp.float32) for b in range(count)], axis=1
        )

    def two_heads(pair, unit, side):
        for b in range(wq.shape[0] // BLOCK):
            rows = slice(b * BLOCK, (b + 1) * BLOCK)
            block = q_all[unit, rows, side * 2 * HEADW : (side + 1) * 2 * HEADW]
            wq[rows, :] = (
                block.astype(jnp.float32) * scale_row(qs_ref, b, 3 * pair, 3)
            ).astype(jnp.bfloat16)
        q = jnp.dot(queries[...], wq[...], preferred_element_type=jnp.float32)
        q = q.astype(jnp.bfloat16).astype(jnp.float32)
        mid, end = q[:, NOPE : 2 * NOPE], q[:, 2 * NOPE :]
        nope = (
            q[:, :NOPE].astype(jnp.bfloat16),
            jnp.where(low_half, pltpu.roll(mid, ROPE, 1), pltpu.roll(end, ROPE, 1)).astype(
                jnp.bfloat16
            ),
        )
        flat = jnp.where(low_half, mid, end)
        swapped = jnp.where(low_quarter, pltpu.roll(flat, 96, 1), pltpu.roll(flat, 32, 1))
        turned = flat * cos_ref[...] + swapped * sin_ref[...]
        ropes = (turned.astype(jnp.bfloat16), pltpu.roll(turned, ROPE, 1).astype(jnp.bfloat16))
        row_id = lax.broadcasted_iota(jnp.int32, (toks, toks), 0)
        col_id = lax.broadcasted_iota(jnp.int32, (toks, toks), 1)
        causal = col_id <= row_id
        outs = []
        scored = []
        for side_head in range(2):
            head = 2 * pair + side_head
            first = pl.multiple_of(head * 2 * BLOCK, 2 * BLOCK)
            wk = (
                kv_all[pl.ds(first, BLOCK), :].astype(jnp.float32)
                * scale_row(ks_ref, 2 * head, 0, LATENT // BLOCK)
            ).astype(jnp.bfloat16)
            wv = (
                kv_all[pl.ds(first + BLOCK, BLOCK), :].astype(jnp.float32)
                * scale_row(ks_ref, 2 * head + 1, 0, LATENT // BLOCK)
            ).astype(jnp.bfloat16)
            lat = jnp.dot(nope[side_head], wk, preferred_element_type=jnp.float32).astype(
                jnp.bfloat16
            )
            full = jnp.concatenate([lat, ropes[side_head]], axis=1)
            dims = (((1,), (1,)), ((), ()))
            s = lax.dot_general(full, keys[...], dims, preferred_element_type=jnp.float32)
            scored.append((s, wv))
        for s, wv in scored:
            s_old = s[:, :prior] + bias_ref[...]
            s_new = jnp.where(causal, s[:, prior:], -jnp.inf)
            top = jnp.maximum(
                jnp.max(s_old, axis=1, keepdims=True), jnp.max(s_new, axis=1, keepdims=True)
            )
            e = jnp.exp2((jnp.concatenate([s_old, s_new], axis=1) - top) * scale)
            w = (e * (1.0 / jnp.sum(e, axis=1, keepdims=True))).astype(jnp.bfloat16)
            mixed = jnp.dot(w, keys[:, :LATENT], preferred_element_type=jnp.float32).astype(
                jnp.bfloat16
            )
            outs.append(
                lax.dot_general(mixed, wv, dims, preferred_element_type=jnp.float32).astype(
                    jnp.bfloat16
                )
            )
        out_ref[:, pl.ds(pl.multiple_of(pair * 2 * VDIM, 2 * VDIM), 2 * VDIM)] = jnp.concatenate(
            outs, axis=1
        )

    for i in range(1, n_mp):
        for copy in row_copies(i):
            copy.start()
    for i in range(1, n_seq):
        page_copy(i).start()
    for u in range(AHEAD):
        send_own(jnp.int32(u))
    for copy in local:
        copy.start()
    for k in range(Q_UNITS):
        own_panel(k).start()

    def step(t, carry):
        relay(t)
        send_own(t + AHEAD)
        share(t - 1)
        collect(t - 1)

        @pl.when(t - 1 == KV_UNITS)
        def _():
            for i in range(1, n_mp):
                row_arrivals(i)
            for i in range(1, n_seq):
                page_arrival(i)
            for copy in local:
                copy.wait()

        @pl.when(t - 1 >= KV_UNITS)
        def _():
            k = t - 1 - KV_UNITS
            own_panel(k).wait()
            two_heads(2 * k, k, 0)
            two_heads(2 * k + 1, k, 1)

        return carry

    lax.fori_loop(0, UNITS + 1, step, 0)

    for i in range(1, n_mp):
        for copy in row_copies(i):
            copy.wait_send()
    for i in range(1, n_seq):
        page_copy(i).wait_send()

    def drain(u, carry):
        sent(u)
        return carry

    lax.fori_loop(0, UNITS, drain, 0)


def fused_body(
    query_latent,
    new_kv,
    q_weight,
    q_scales,
    kv_weight,
    kv_scales,
    kv_gain,
    pool_latent,
    pool_rope,
    page_table,
    prior_len,
):
    seq_count = lax.axis_size("seq")
    mp_count = lax.axis_size("mp")
    own_index = lax.axis_index("seq")
    mp_index = lax.axis_index("mp")
    own_rows = query_latent.shape[0]
    toks = own_rows * mp_count
    page_count = page_table.shape[1]
    pool_count, page_len = pool_latent.shape[:2]
    length = lax.dynamic_index_in_dim(prior_len, own_index, 0, keepdims=False)
    cosine, sine = rope_tables(length + jnp.arange(toks, dtype=jnp.int32))
    cos_table = jnp.tile(cosine, (1, 4))
    sin_table = jnp.tile(jnp.concatenate([-sine, sine], axis=1), (1, 2))

    first = mp_index * own_rows
    own_cos = lax.dynamic_slice_in_dim(cosine, first, own_rows, 0)
    own_sin = lax.dynamic_slice_in_dim(sine, first, own_rows, 0)
    latent_part = new_kv[:, :LATENT].astype(jnp.float32)
    inv_rms = lax.rsqrt(jnp.mean(latent_part * latent_part, axis=-1, keepdims=True) + NORM_EPS)
    new_lat = latent_part * inv_rms * kv_gain[None, :]
    new_rope = rotate(new_kv[:, LATENT:].astype(jnp.float32), own_cos, own_sin)
    new_keys = jnp.concatenate([new_lat, new_rope, jnp.zeros_like(new_rope)], axis=1).astype(
        jnp.bfloat16
    )

    holders = page_table // pool_count
    pool_slots = page_table % pool_count
    earlier = jnp.arange(page_count)[None, :] < jnp.arange(page_count)[:, None]
    same_holder = holders[:, :, None] == holders[:, None, :]
    page_ranks = jnp.sum(jnp.where(same_holder & earlier[None], 1, 0), axis=2)
    capacity = (page_count + seq_count - 1) // seq_count
    wanted = (holders[:, None, :] == own_index) & (
        page_ranks[:, None, :] == jnp.arange(capacity)[None, :, None]
    )
    send_slot = jnp.sum(jnp.where(wanted, pool_slots[:, None, :], 0), axis=2).reshape(-1)
    rope_rows = pool_rope.reshape(pool_count, page_len, ROPE)
    pool_keys = jnp.concatenate([pool_latent, rope_rows, jnp.zeros_like(rope_rows)], axis=2)
    pages = pool_keys[send_slot].reshape(seq_count, capacity * page_len, KEYW)

    own_place = lax.dynamic_index_in_dim(holders * capacity + page_ranks, own_index, 0, False)
    at_slot = own_place[None, :] == jnp.arange(seq_count * capacity)[:, None]
    slot_page = jnp.sum(jnp.where(at_slot, jnp.arange(page_count)[None, :], 0), axis=1)
    slot_page = jnp.where(jnp.any(at_slot, axis=1), slot_page, page_count)
    token = slot_page[:, None] * page_len + jnp.arange(page_len)[None, :]
    seen = token < jnp.minimum(length, page_count * page_len)
    bias = jnp.where(seen, 0.0, -jnp.inf).astype(jnp.float32).reshape(1, -1)

    prior = seq_count * capacity * page_len
    heads = q_weight.shape[1] // HEADW
    anywhere = pl.BlockSpec(memory_space=pl.ANY)
    vmem = pl.BlockSpec(memory_space=pltpu.VMEM)
    smem = pl.BlockSpec(memory_space=pltpu.SMEM)
    return pl.pallas_call(
        fused_kernel,
        out_shape=jax.ShapeDtypeStruct((toks, heads * VDIM), jnp.bfloat16),
        in_specs=[anywhere] * 5 + [smem] * 2 + [vmem] * 3,
        out_specs=vmem,
        scratch_shapes=[
            pltpu.VMEM(
                (Q_UNITS, q_weight.shape[0] * seq_count, q_weight.shape[1] // Q_UNITS),
                jnp.bfloat16,
            ),
            pltpu.VMEM((kv_weight.shape[0] * seq_count, LATENT), jnp.bfloat16),
            pltpu.VMEM((prior + toks, KEYW), jnp.bfloat16),
            pltpu.VMEM((toks, query_latent.shape[1]), jnp.bfloat16),
            pltpu.VMEM((q_weight.shape[0] * seq_count, 2 * HEADW), jnp.bfloat16),
            pltpu.SemaphoreType.DMA((UNITS * LANES,)),
            pltpu.SemaphoreType.DMA((UNITS * LANES,)),
            pltpu.SemaphoreType.DMA((seq_count,)),
            pltpu.SemaphoreType.DMA((seq_count,)),
            pltpu.SemaphoreType.DMA((2 * mp_count,)),
            pltpu.SemaphoreType.DMA((2 * mp_count,)),
            pltpu.SemaphoreType.DMA((Q_UNITS + 4,)),
        ],
        compiler_params=pltpu.CompilerParams(
            collective_id=0, has_side_effects=True, vmem_limit_bytes=56 * 1024 * 1024
        ),
        cost_estimate=pl.CostEstimate(
            flops=30 * 10**9, bytes_accessed=10**7, transcendentals=10**7
        ),
    )(
        query_latent,
        new_keys,
        pages,
        q_weight,
        kv_weight,
        q_scales,
        kv_scales,
        cos_table,
        sin_table,
        bias,
    )


def solution(mesh):
    in_specs = (
        P(("seq", "mp"), None),
        P(("seq", "mp"), None),
        P("seq", "mp"),
        P(None, "mp"),
        P(("mp", "seq"), None),
        P("mp", None),
        P(),
        P("seq", None, None),
        P("seq", None),
        P(),
        P(),
    )
    out_specs = P("seq", "mp")
    fused = mesh.shape["seq"] == 8 and mesh.shape["mp"] == 4
    return jax.shard_map(
        fused_body if fused else body,
        mesh=mesh,
        in_specs=in_specs,
        out_specs=out_specs,
        check_vma=False,
    )
```
